512 devices in a mesh: gx: 8 (over y, core), gy: 4 (over z_hi), gz: 16 (over z_lo, x).
Axes of the slice: x: 4, y: 4, z: 16 (z_hi: 4, z_lo: 4; z = z_hi * 4 + z_lo), core: 2. Of those that a mesh axis runs over, the one named last changes fastest.
Arguments:
- inputs: bfloat16 [24576, 7168], P(('gy', 'gx'), 'gz'), may hold values from -6 to 6
- out_grads: bfloat16 [24576, 8192], P(('gy', 'gz'), 'gx'), may hold values from -0.0390625 to 0.0390625
- weights: bfloat16 [7168, 8192], P(('gz', 'gy'), 'gx'), may hold values from -0.29882812 to 0.29882812
- first_moment: float32 [7168, 8192], P(('gz', 'gy'), 'gx'), may hold values from -3 to 3
- second_moment: float32 [7168, 8192], P(('gz', 'gy'), 'gx'), may hold values from 0.05 to 2
Outputs:
- first_next: float32 [7168, 8192], P(('gz', 'gy'), 'gx')
- second_next: float32 [7168, 8192], P(('gz', 'gy'), 'gx')
- weight_next: bfloat16 [7168, 8192], P('gz', 'gx')
The draws below stay inside these ranges and needn't reach their ends.
All inputs are finite; a program needn't handle non-finite values.
Results may differ from the reference program's by a relative error of at most 0.004.
Values may be sent and summed in bfloat16 or wider, within the bound.
A program may use at most 64 MiB of HBM per device.

```python
import math
import jax
import jax.numpy as jnp
from jax import lax

D = 7168
F = 8192
TOKENS = 24576


def shard_levels(stream_key, dims, split, low, high):
    def one(axis_at, blocks):
        steps = jax.random.uniform(jax.random.fold_in(jax.random.fold_in(stream_key, 6), axis_at), (blocks,), jnp.float32, low / len(split), high / len(split))
        return jnp.repeat(jnp.exp(steps), dims[axis_at] // blocks).reshape((-1,) + (1,) * (len(dims) - axis_at - 1))

    loudness = one(*split[0])
    for cut in split[1:]:
        loudness = loudness * one(*cut)
    return loudness


def normal_values(stream_key, shape, scale, reach, pieces=(), held_as=jnp.bfloat16):
    gain = shard_levels(stream_key, shape, pieces, -0.22, 0.18) if pieces else 1.0
    values = jax.random.normal(stream_key, shape, jnp.float32) * scale * gain
    return jnp.minimum(jnp.maximum(values, -reach), reach).astype(held_as)


def setup_inputs(seed: int = 0) -> dict:
    seeds = jax.random.split(jax.random.key(seed), 6)
    inputs = normal_values(seeds[0], (TOKENS, D), 1.0, 6.0, ((0, 32), (1, 16)))
    out_grads = normal_values(seeds[1], (TOKENS, F), TOKENS ** -0.5, 0.0390625, ((0, 64), (1, 8)))
    weights = normal_values(seeds[2], (D, F), 0.05, 0.29882812, ((0, 64), (1, 8)))
    first_moment = normal_values(seeds[3], (D, F), 0.5, 3.0, ((0, 64), (1, 8)), jnp.float32)
    second_moment = jnp.clip(jnp.exp(math.log(2.0) - 3.6888794 * jax.random.uniform(seeds[4], (D, F), jnp.float32) ** shard_levels(seeds[4], (D, F), ((0, 64), (1, 8)), -0.2, 0.2)), 0.05, 2.0)
    return {"inputs": inputs, "out_grads": out_grads, "weights": weights, "first_moment": first_moment, "second_moment": second_moment}


beta_one = 0.9
beta_two = 0.95
adam_step = 10.0
learn_rate = 0.01
decay_rate = 0.1
epsilon = 1e-08

def reference(inputs, out_grads, weights, first_moment, second_moment):
    grad = lax.dot_general(inputs, out_grads, (((0,), (0,)), ((), ())), preferred_element_type=jnp.float32)
    first_next = beta_one * first_moment + (1.0 - beta_one) * grad
    second_next = beta_two * second_moment + (1.0 - beta_two) * grad * grad
    corr_one = 1.0 - beta_one ** adam_step
    corr_two = 1.0 - beta_two ** adam_step
    update = first_next / corr_one / (jnp.sqrt(second_next / corr_two) + epsilon) + decay_rate * weights.astype(jnp.float32)
    weight_next = (weights.astype(jnp.float32) - learn_rate * update).astype(jnp.bfloat16)
    return (first_next, second_next, weight_next)
```

```python
import functools
import jax
import jax.numpy as jnp
from jax import lax
from jax.experimental import pallas as pl
from jax.experimental.pallas import tpu as pltpu
from jax.sharding import PartitionSpec as P

beta_one = 0.9
beta_two = 0.95
adam_step = 10.0
learn_rate = 0.01
decay_rate = 0.1
epsilon = 1e-08

BF = jnp.bfloat16
F32 = jnp.float32

RING = 16
ROWS = 112
HALF = 768
PART = 384
COLS = 1024
CHAINS = 4
WIDE = COLS // CHAINS


def kernel(a_ref, b_ref, w_ref, m1_ref, m2_ref, m1n_ref, m2n_ref, wn_ref,
           at_own, at_all, b_all, part, recv, send,
           a1_s, a1_r, loc, ym_s, yp_s, ym_r, yp_r, rm_s, rp_s, rm_r, rp_r,
           sib_s, sib_r, b_s, b_r, rs_s, rs_r, up_s, dn_s, up_r, dn_r, fw_s, fw_r):
    gx, h, gz = lax.axis_index("gx"), lax.axis_index("gy"), lax.axis_index("gz")
    y, c = gx // 2, gx % 2
    l, x = gz // 4, gz % 4
    z = 4 * h + l

    def dev(y_=y, c_=c, z_=z, x_=x):
        return {"gx": 2 * y_ + c_, "gy": z_ // 4, "gz": 4 * (z_ % 4) + x_}

    def remote(src, dst, s, r, to):
        return pltpu.make_async_remote_copy(
            src_ref=src, dst_ref=dst, send_sem=s, recv_sem=r,
            device_id=to, device_id_type=pl.DeviceIdType.MESH)

    y_up, y_dn, y_far = (y + 1) % 4, (y + 3) % 4, (y + 2) % 4
    z_up, z_dn = (z + 1) % RING, (z + RING - 1) % RING
    z_up4, z_dn4 = (z + 4) % RING, (z + RING - 4) % RING
    near = [dev(x_=(x + 1) % 4), dev(x_=(x + 3) % 4), dev(x_=(x + 2) % 4),
            dev(y_=y_up), dev(y_=y_dn), dev(c_=1 - c),
            dev(z_=z_up), dev(z_=z_dn), dev(z_=z_up4), dev(z_=z_dn4)]

    barrier = pltpu.get_barrier_semaphore()
    for to in near:
        pl.semaphore_signal(barrier, inc=1, device_id=to, device_id_type=pl.DeviceIdType.MESH)
    for i in range(4):
        @pl.when(jnp.logical_or(y != l, i != l))
        def _():
            pl.semaphore_signal(barrier, inc=1, device_id=dev(y_=l, z_=4 * h + i),
                                device_id_type=pl.DeviceIdType.MESH)
    at_own[...] = a_ref[...].T
    own_b = pltpu.make_async_copy(b_ref, b_all.at[x], loc.at[0])
    own_b.start()
    pl.semaphore_wait(barrier, len(near) + 4 - jnp.where(y == l, 1, 0))

    b_copies = [remote(b_ref, b_all.at[x], b_s.at[i], b_r.at[i], near[i]) for i in range(3)]
    a1 = [remote(at_own.at[pl.ds(ROWS * k, ROWS), :], at_all.at[l, k, c], a1_s.at[k], a1_r.at[l],
                 dev(y_=k, z_=4 * h + y)) for k in range(4)]
    stay = pltpu.make_async_copy(at_own.at[pl.ds(pl.multiple_of(ROWS * y, 16), ROWS), :],
                                 at_all.at[l, y, c], loc.at[1])
    for k in range(4):
        @pl.when(jnp.logical_or(y != l, k != y))
        def _():
            a1[k].start()

    @pl.when(y == l)
    def _():
        stay.start()
    for copy in b_copies:
        copy.start()

    order = [(l + 3) % 4, (l + 1) % 4, l, (l + 2) % 4]

    def hand_on(i, k):
        piece = at_all.at[i, k, c]
        return remote(piece, piece, sib_s.at[i, k], sib_r.at[i, k], dev(c_=1 - c))

    def to_up(i):
        piece = at_all.at[i, y, c]
        return remote(piece, piece, yp_s.at[i], yp_r.at[i], dev(y_=y_up))

    def to_dn(i):
        piece = at_all.at[i, y, c]
        return remote(piece, piece, ym_s.at[i], ym_r.at[i], dev(y_=y_dn))

    def relay_up(i, k):
        piece = at_all.at[i, k, c, :, pl.ds(0, HALF // 2)]
        return remote(piece, piece, rp_s.at[i], rp_r.at[i], dev(y_=y_up))

    def relay_dn(i, k):
        piece = at_all.at[i, k, c, :, pl.ds(HALF // 2, HALF // 2)]
        return remote(piece, piece, rm_s.at[i], rm_r.at[i], dev(y_=y_dn))

    for i in order:
        @pl.when(jnp.logical_or(y != l, i != l))
        def _():
            remote(at_all.at[i, y, c], at_all.at[i, y, c], a1_s.at[0], a1_r.at[i], near[0]).wait_recv()

        @pl.when(jnp.logical_and(y == l, i == l))
        def _():
            stay.wait()
        to_up(i).start()
        to_dn(i).start()
        hand_on(i, y).start()

    for i in order:
        remote(at_all.at[i, y_dn, c], at_all.at[i, y_dn, c], yp_s.at[i], yp_r.at[i], near[0]).wait_recv()
        relay_up(i, y_dn).start()
        hand_on(i, y_dn).start()
        remote(at_all.at[i, y_up, c], at_all.at[i, y_up, c], ym_s.at[i], ym_r.at[i], near[0]).wait_recv()
        relay_dn(i, y_up).start()
        hand_on(i, y_up).start()
    for i in order:
        relay_up(i, y_far).wait_recv()
        relay_dn(i, y_far).wait_recv()
        hand_on(i, y_far).start()

    own_b.wait()
    for i, q in enumerate([(x + 3) % 4, (x + 1) % 4, (x + 2) % 4]):
        remote(b_ref, b_all.at[q], b_s.at[i], b_r.at[i], near[i]).wait_recv()

    for i in order:
        for k in range(4):
            hand_on(i, k).wait_recv()

        @pl.loop(0, CHAINS)
        def _(j):
            cols = pl.ds(pl.multiple_of(j * WIDE, WIDE), WIDE)
            total = jnp.zeros((4 * ROWS, WIDE), F32)
            for core in range(2):
                left = at_all[i, :, core].reshape(4 * ROWS, HALF)
                right = b_all[pl.ds(2 * core, 2), :, cols].reshape(HALF, WIDE)
                total += jnp.dot(left, right, preferred_element_type=F32)
            part[i, :, :, cols] = total.reshape(4, ROWS, WIDE)

    def block(chain, s):
        d = (z + RING - 1 - s) % RING if chain < CHAINS // 2 else (z + 1 + s) % RING
        return part[d % 4, d // 4, :, pl.ds(chain * WIDE, WIDE)]

    def hop(chain, s):
        to = z_up if chain < CHAINS // 2 else z_dn
        return remote(send.at[chain, s], recv.at[chain, s], rs_s.at[chain, s], rs_r.at[chain, s], dev(z_=to))

    for chain in range(CHAINS):
        send[chain, 0] = block(chain, 0).astype(BF)
        hop(chain, 0).start()

    def ring_step(s, carry):
        for chain in range(CHAINS):
            mine = block(chain, s)
            hop(chain, s - 1).wait_recv()
            send[chain, s] = (mine + recv[chain, s - 1].astype(F32)).astype(BF)
            hop(chain, s).start()
        return carry

    lax.fori_loop(1, RING - 1, ring_step, 0)

    def weights_up(f):
        piece = wn_ref.at[h, :, pl.ds(f * WIDE, WIDE)]
        return remote(piece, piece, up_s.at[f], up_r.at[f], dev(z_=z_up4))

    def weights_dn(f):
        piece = wn_ref.at[h, :, pl.ds(f * WIDE, WIDE)]
        return remote(piece, piece, dn_s.at[f], dn_r.at[f], dev(z_=z_dn4))

    corr_one = 1.0 - beta_one**adam_step
    corr_two = 1.0 - beta_two**adam_step
    for chain in [0, 2, 1, 3]:
        cols = pl.ds(chain * WIDE, WIDE)
        mine = block(chain, RING - 1)
        hop(chain, RING - 2).wait_recv()
        grad = mine + recv[chain, RING - 2].astype(F32)
        first_next = beta_one * m1_ref[:, cols] + (1.0 - beta_one) * grad
        second_next = beta_two * m2_ref[:, cols] + (1.0 - beta_two) * grad * grad
        m1n_ref[:, cols] = first_next
        m2n_ref[:, cols] = second_next
        wide = w_ref[:, cols].astype(F32)
        update = (first_next / corr_one / (jnp.sqrt(second_next / corr_two) + epsilon)
                  + decay_rate * wide)
        wn_ref[h, :, cols] = (wide - learn_rate * update).astype(BF)
        weights_up(chain).start()
        weights_dn(chain).start()

    h_dn, h_up, h_far = (h + 3) % 4, (h + 1) % 4, (h + 2) % 4

    def pass_up(f, k):
        piece = wn_ref.at[k, :, pl.ds(f * WIDE, WIDE)]
        return remote(piece, piece, fw_s.at[f], fw_r.at[f], dev(z_=z_up4))

    def pass_dn(f, k):
        piece = wn_ref.at[k, :, pl.ds(f * WIDE, WIDE)]
        return remote(piece, piece, fw_s.at[f], fw_r.at[f], dev(z_=z_dn4))

    for f in [0, 2, 1, 3]:
        if f < CHAINS // 2:
            weights_up(f).wait_recv()
            pass_up(f, h_dn).start()
        else:
            weights_dn(f).wait_recv()
            pass_dn(f, h_up).start()
    for f in range(CHAINS):
        if f < CHAINS // 2:
            weights_dn(f).wait_recv()
        else:
            weights_up(f).wait_recv()
        pass_up(f, h_far).wait_recv()

    for copy in b_copies:
        copy.wait_send()
    for k in range(4):
        @pl.when(jnp.logical_or(y != l, k != y))
        def _():
            a1[k].wait_send()
    for i in range(4):
        to_up(i).wait_send()
        to_dn(i).wait_send()
        relay_up(i, 0).wait_send()
        relay_dn(i, 0).wait_send()
        for k in range(4):
            hand_on(i, k).wait_send()
    for chain in range(CHAINS):
        weights_up(chain).wait_send()
        weights_dn(chain).wait_send()
        pass_up(chain, 0).wait_send()

    def drain(s, carry):
        for chain in range(CHAINS):
            hop(chain, s).wait_send()
        return carry

    lax.fori_loop(0, RING - 1, drain, 0)


def body(inputs, out_grads, weights, first_moment, second_moment):
    vmem = pl.BlockSpec(memory_space=pltpu.VMEM)
    dma = pltpu.SemaphoreType.DMA
    own = first_moment.shape
    first_next, second_next, weight_next = pl.pallas_call(
        kernel,
        name="adam_grad",
        out_shape=(jax.ShapeDtypeStruct(own, F32), jax.ShapeDtypeStruct(own, F32),
                   jax.ShapeDtypeStruct((4, ROWS, COLS), BF)),
        in_specs=[vmem] * 5,
        out_specs=(vmem,) * 3,
        scratch_shapes=[
            pltpu.VMEM((4 * ROWS, HALF), BF),
            pltpu.VMEM((4, 4, 2, ROWS, HALF), BF),
            pltpu.VMEM((4, PART, COLS), BF),
            pltpu.VMEM((4, 4, ROWS, COLS), F32),
            pltpu.VMEM((CHAINS, RING - 1, ROWS, WIDE), BF),
            pltpu.VMEM((CHAINS, RING - 1, ROWS, WIDE), BF),
            dma((4,)), dma((4,)), dma((2,)),
            dma((4,)), dma((4,)), dma((4,)), dma((4,)),
            dma((4,)), dma((4,)), dma((4,)), dma((4,)),
            dma((4, 4)), dma((4, 4)),
            dma((3,)), dma((3,)),
            dma((CHAINS, RING - 1)), dma((CHAINS, RING - 1)),
            dma((CHAINS,)), dma((CHAINS,)), dma((CHAINS,)), dma((CHAINS,)),
            dma((CHAINS,)), dma((CHAINS,)),
        ],
        compiler_params=pltpu.CompilerParams(
            collective_id=0, has_side_effects=True, vmem_limit_bytes=48 * 2**20),
        cost_estimate=pl.CostEstimate(flops=5_700_000_000, bytes_accessed=6_000_000, transcendentals=0),
    )(inputs, out_grads, weights, first_moment, second_moment)
    return first_next, second_next, weight_next.reshape(4 * ROWS, COLS)


def solution(mesh):
    in_specs = (
        P(("gy", "gx"), "gz"),
        P(("gy", "gz"), "gx"),
        P(("gz", "gy"), "gx"),
        P(("gz", "gy"), "gx"),
        P(("gz", "gy"), "gx"),
    )
    out_specs = (P(("gz", "gy"), "gx"), P(("gz", "gy"), "gx"), P("gz", "gx"))
    return jax.shard_map(body, mesh=mesh, in_specs=in_specs, out_specs=out_specs, check_vma=False)
```

```python
import functools
import jax
import jax.numpy as jnp
from jax import lax
from jax.experimental import pallas as pl
from jax.experimental.pallas import tpu as pltpu
from jax.sharding import PartitionSpec as P

beta_one = 0.9
beta_two = 0.95
adam_step = 10.0
learn_rate = 0.01
decay_rate = 0.1
epsilon = 1e-08

BF = jnp.bfloat16
F32 = jnp.float32

RING = 16
ROWS = 112
HALF = 768
PART = 384
COLS = 1024
CHAINS = 8
WIDE = COLS // CHAINS
SENDS = 4
TILE = 256


def kernel(a_ref, b_ref, w_ref, m1_ref, m2_ref, m1n_ref, m2n_ref, wn_ref,
           own, moved, at_all, b_all, part, recv, send,
           sc_s, sc_r, zm_s, zm_r, loc, ym_s, yp_s, ym_r, yp_r, rm_s, rp_s, rm_r, rp_r,
           sib_s, sib_r, b_s, b_r, rs_s, rs_r, up_s, dn_s, up_r, dn_r, fw_s, fw_r):
    gx, h, gz = lax.axis_index("gx"), lax.axis_index("gy"), lax.axis_index("gz")
    y, c = gx // 2, gx % 2
    l, x = gz // 4, gz % 4
    z = 4 * h + l

    def dev(y_=y, c_=c, z_=z, x_=x):
        return {"gx": 2 * y_ + c_, "gy": z_ // 4, "gz": 4 * (z_ % 4) + x_}

    def remote(src, dst, s, r, to):
        return pltpu.make_async_remote_copy(
            src_ref=src, dst_ref=dst, send_sem=s, recv_sem=r,
            device_id=to, device_id_type=pl.DeviceIdType.MESH)

    x_up, x_dn, x_far = (x + 1) % 4, (x + 3) % 4, (x + 2) % 4
    y_up, y_dn, y_far = (y + 1) % 4, (y + 3) % 4, (y + 2) % 4
    z_up, z_dn = (z + 1) % RING, (z + RING - 1) % RING
    z_up4, z_dn4 = (z + 4) % RING, (z + RING - 4) % RING
    near = [dev(x_=x_up), dev(x_=x_dn), dev(y_=y_up), dev(y_=y_dn), dev(y_=y_far), dev(c_=1 - c),
            dev(z_=z_up), dev(z_=z_dn), dev(z_=z_up4), dev(z_=z_dn4)]
    near += [dev(z_=4 * h + (l + i) % 4) for i in (1, 2, 3)]

    barrier = pltpu.get_barrier_semaphore()
    for to in near:
        pl.semaphore_signal(barrier, inc=1, device_id=to, device_id_type=pl.DeviceIdType.MESH)
    own[...] = a_ref[...].T.reshape(4, ROWS, HALF)
    own_b = pltpu.make_async_copy(b_ref, b_all.at[x], loc.at[0])
    own_b.start()
    pl.semaphore_wait(barrier, len(near))

    mine_at = pl.multiple_of(c * HALF, 128)

    def held(i, k, first=0, wide=HALF):
        return at_all.at[i, k, :, pl.ds(pl.multiple_of(mine_at + first, 128), wide)]

    def scatter(dk, stays):
        k = (y + dk) % 4
        return remote(own.at[k], held(l, k) if stays else moved.at[y], sc_s.at[dk - 1], sc_r.at[dk - 1], dev(y_=k))

    def z_move(i, src, p):
        return remote(src, held(l, y), zm_s.at[i], zm_r.at[l], dev(z_=4 * h + p))

    stay = pltpu.make_async_copy(own.at[y], held(l, y), loc.at[1])

    @pl.when(y == l)
    def _():
        stay.start()
        for dk in (1, 3, 2):
            scatter(dk, True).start()

    @pl.when(y != l)
    def _():
        z_move(0, own.at[y], y).start()
        for dk in (1, 3, 2):
            scatter(dk, False).start()

    def b_up():
        return remote(b_ref, b_all.at[x], b_s.at[0], b_r.at[0], dev(x_=x_up))

    def b_dn():
        return remote(b_ref, b_all.at[x], b_s.at[1], b_r.at[1], dev(x_=x_dn))

    def b_on_up(q):
        piece = b_all.at[q, pl.ds(0, PART // 2), :]
        return remote(piece, piece, b_s.at[2], b_r.at[2], dev(x_=x_up))

    def b_on_dn(q):
        piece = b_all.at[q, pl.ds(PART // 2, PART // 2), :]
        return remote(piece, piece, b_s.at[3], b_r.at[3], dev(x_=x_dn))

    b_up().start()
    b_dn().start()

    for dk in (1, 3, 2):
        p = (y + 4 - dk) % 4
        scatter(dk, False).wait_recv()

        @pl.when(p != l)
        def _():
            z_move(dk, moved.at[p], p).start()

    mirror = l // 2
    near_l = jnp.where(mirror == 1, 3 - l, l)
    order = [jnp.where(mirror == 1, 3 - i, i) for i in (near_l, 1 - near_l, 2, 3)]

    def hand_on(i, k):
        return remote(held(i, k), held(i, k), sib_s.at[i, k], sib_r.at[i, k], dev(c_=1 - c))

    def to_up(i):
        return remote(held(i, y), held(i, y), yp_s.at[i], yp_r.at[i], dev(y_=y_up))

    def to_dn(i):
        return remote(held(i, y), held(i, y), ym_s.at[i], ym_r.at[i], dev(y_=y_dn))

    def relay_up(i, k):
        piece = held(i, k, 0, HALF // 2)
        return remote(piece, piece, rp_s.at[i], rp_r.at[i], dev(y_=y_up))

    def relay_dn(i, k):
        piece = held(i, k, HALF // 2, HALF // 2)
        return remote(piece, piece, rm_s.at[i], rm_r.at[i], dev(y_=y_dn))

    def share(i):
        to_up(i).start()
        to_dn(i).start()
        hand_on(i, y).start()

    def relay(i):
        to_up(i).wait_recv()
        relay_up(i, y_dn).start()
        hand_on(i, y_dn).start()
        to_dn(i).wait_recv()
        relay_dn(i, y_up).start()
        hand_on(i, y_up).start()

    def far(i):
        relay_up(i, y_far).wait_recv()
        relay_dn(i, y_far).wait_recv()
        hand_on(i, y_far).start()

    @pl.when(y == l)
    def _():
        stay.wait()

    share(order[0])
    for n in (1, 2, 3):
        remote(own.at[0], held(order[n], y), zm_s.at[0], zm_r.at[order[n]], dev(c_=1 - c)).wait_recv()
        share(order[n])
        relay(order[n - 1])
        if n == 2:
            b_up().wait_recv()
            b_on_up(x_dn).start()
            b_dn().wait_recv()
            b_on_dn(x_up).start()
        if n >= 2:
            far(order[n - 2])
    relay(order[3])
    far(order[2])

    own_b.wait()
    b_on_up(x_far).wait_recv()
    b_on_dn(x_far).wait_recv()

    for n in range(4):
        i = order[n]
        if n == 1:
            far(order[3])
        for k in range(4):
            hand_on(i, k).wait_recv()

        @pl.loop(0, COLS // TILE)
        def _(j):
            cols = pl.ds(pl.multiple_of(j * TILE, TILE), TILE)
            total = jnp.dot(at_all[i].reshape(4 * ROWS, 2 * HALF), b_all[:, :, cols].reshape(2 * HALF, TILE),
                            preferred_element_type=F32)
            part[i, :, :, cols] = total.reshape(4, ROWS, TILE)

    def block(chain, s):
        d = (z + RING - 1 - s) % RING if chain < CHAINS // 2 else (z + 1 + s) % RING
        return part[d % 4, d // 4, :, pl.ds(chain * WIDE, WIDE)]

    def hop(chain, s):
        to = z_up if chain < CHAINS // 2 else z_dn
        return remote(send.at[chain, s], recv.at[chain, s], rs_s.at[chain, s], rs_r.at[chain, s], dev(z_=to))

    for chain in range(CHAINS):
        send[chain, 0] = block(chain, 0).astype(BF)
        hop(chain, 0).start()

    def ring_step(s, carry):
        for chain in range(CHAINS):
            mine = block(chain, s)
            hop(chain, s - 1).wait_recv()
            send[chain, s] = (mine + recv[chain, s - 1].astype(F32)).astype(BF)
            hop(chain, s).start()
        return carry

    lax.fori_loop(1, RING - 1, ring_step, 0)

    def weights(f, k):
        return wn_ref.at[k, :, pl.ds(f * (COLS // SENDS), COLS // SENDS)]

    def weights_up(f):
        return remote(weights(f, h), weights(f, h), up_s.at[f], up_r.at[f], dev(z_=z_up4))

    def weights_dn(f):
        return remote(weights(f, h), weights(f, h), dn_s.at[f], dn_r.at[f], dev(z_=z_dn4))

    corr_one = 1.0 - beta_one**adam_step
    corr_two = 1.0 - beta_two**adam_step
    for chain in [0, 1, 4, 5, 2, 3, 6, 7]:
        cols = pl.ds(chain * WIDE, WIDE)
        mine = block(chain, RING - 1)
        hop(chain, RING - 2).wait_recv()
        grad = mine + recv[chain, RING - 2].astype(F32)
        first_next = beta_one * m1_ref[:, cols] + (1.0 - beta_one) * grad
        second_next = beta_two * m2_ref[:, cols] + (1.0 - beta_two) * grad * grad
        m1n_ref[:, cols] = first_next
        m2n_ref[:, cols] = second_next
        wide = w_ref[:, cols].astype(F32)
        update = (first_next / corr_one / (jnp.sqrt(second_next / corr_two) + epsilon)
                  + decay_rate * wide)
        wn_ref[h, :, cols] = (wide - learn_rate * update).astype(BF)
        if chain % 2 == 1:
            weights_up(chain // 2).start()
            weights_dn(chain // 2).start()

    h_dn, h_up, h_far = (h + 3) % 4, (h + 1) % 4, (h + 2) % 4

    def pass_up(f, k):
        return remote(weights(f, k), weights(f, k), fw_s.at[f], fw_r.at[f], dev(z_=z_up4))

    def pass_dn(f, k):
        return remote(weights(f, k), weights(f, k), fw_s.at[f], fw_r.at[f], dev(z_=z_dn4))

    for f in [0, 2, 1, 3]:
        if f < SENDS // 2:
            weights_up(f).wait_recv()
            pass_up(f, h_dn).start()
        else:
            weights_dn(f).wait_recv()
            pass_dn(f, h_up).start()
    for f in range(SENDS):
        if f < SENDS // 2:
            weights_dn(f).wait_recv()
        else:
            weights_up(f).wait_recv()
        pass_up(f, h_far).wait_recv()

    b_up().wait_send()
    b_dn().wait_send()
    b_on_up(x_dn).wait_send()
    b_on_dn(x_up).wait_send()
    for dk in (1, 2, 3):
        scatter(dk, False).wait_send()

        @pl.when((y + 4 - dk) % 4 != l)
        def _():
            z_move(dk, moved.at[0], l).wait_send()

    @pl.when(y != l)
    def _():
        z_move(0, own.at[y], l).wait_send()
    for i in range(4):
        to_up(i).wait_send()
        to_dn(i).wait_send()
        relay_up(i, 0).wait_send()
        relay_dn(i, 0).wait_send()
        for k in range(4):
            hand_on(i, k).wait_send()
    for f in range(SENDS):
        weights_up(f).wait_send()
        weights_dn(f).wait_send()
        pass_up(f, 0).wait_send()

    def drain(s, carry):
        for chain in range(CHAINS):
            hop(chain, s).wait_send()
        return carry

    lax.fori_loop(0, RING - 1, drain, 0)


def body(inputs, out_grads, weights, first_moment, second_moment):
    vmem = pl.BlockSpec(memory_space=pltpu.VMEM)
    dma = pltpu.SemaphoreType.DMA
    own = first_moment.shape
    first_next, second_next, weight_next = pl.pallas_call(
        kernel,
        name="adam_grad",
        out_shape=(jax.ShapeDtypeStruct(own, F32), jax.ShapeDtypeStruct(own, F32),
                   jax.ShapeDtypeStruct((4, ROWS, COLS), BF)),
        in_specs=[vmem] * 5,
        out_specs=(vmem,) * 3,
        scratch_shapes=[
            pltpu.VMEM((4, ROWS, HALF), BF),
            pltpu.VMEM((4, ROWS, HALF), BF),
            pltpu.VMEM((4, 4, ROWS, 2 * HALF), BF),
            pltpu.VMEM((4, PART, COLS), BF),
            pltpu.VMEM((4, 4, ROWS, COLS), F32),
            pltpu.VMEM((CHAINS, RING - 1, ROWS, WIDE), BF),
            pltpu.VMEM((CHAINS, RING - 1, ROWS, WIDE), BF),
            dma((3,)), dma((3,)), dma((4,)), dma((4,)), dma((2,)),
            dma((4,)), dma((4,)), dma((4,)), dma((4,)),
            dma((4,)), dma((4,)), dma((4,)), dma((4,)),
            dma((4, 4)), dma((4, 4)),
            dma((4,)), dma((4,)),
            dma((CHAINS, RING - 1)), dma((CHAINS, RING - 1)),
            dma((SENDS,)), dma((SENDS,)), dma((SENDS,)), dma((SENDS,)),
            dma((SENDS,)), dma((SENDS,)),
        ],
        compiler_params=pltpu.CompilerParams(
            collective_id=0, has_side_effects=True, vmem_limit_bytes=48 * 2**20),
        cost_estimate=pl.CostEstimate(flops=5_700_000_000, bytes_accessed=6_000_000, transcendentals=0),
    )(inputs, out_grads, weights, first_moment, second_moment)
    return first_next, second_next, weight_next.reshape(4 * ROWS, COLS)


def solution(mesh):
    in_specs = (
        P(("gy", "gx"), "gz"),
        P(("gy", "gz"), "gx"),
        P(("gz", "gy"), "gx"),
        P(("gz", "gy"), "gx"),
        P(("gz", "gy"), "gx"),
    )
    out_specs = (P(("gz", "gy"), "gx"), P(("gz", "gy"), "gx"), P("gz", "gx"))
    return jax.shard_map(body, mesh=mesh, in_specs=in_specs, out_specs=out_specs, check_vma=False)
```

```python
import functools
import jax
import jax.numpy as jnp
from jax import lax
from jax.experimental import pallas as pl
from jax.experimental.pallas import tpu as pltpu
from jax.sharding import PartitionSpec as P

beta_one = 0.9
beta_two = 0.95
adam_step = 10.0
learn_rate = 0.01
decay_rate = 0.1
epsilon = 1e-08

BF = jnp.bfloat16
F32 = jnp.float32

RING = 16
ROWS = 112
HALF = 768
PART = 384
COLS = 1024
CHUNKS = 4
WIDE = COLS // CHUNKS
REACH = 8
TILE = 256


def kernel(a_ref, b_ref, w_ref, m1_ref, m2_ref, grad_ref, wn_ref,
           moved, at_all, b_all, part, recv, send, w_own, m1_own, m2_own,
           sc_s, sc_r, zm_s, zm_r, loc, ym_s, yp_s, ym_r, yp_r, rm_s, rp_s, rm_r, rp_r,
           sib_s, sib_r, b_s, b_r, rs_s, rs_r, up_s, dn_s, up_r, dn_r, fw_s, fw_r):
    gx, h, gz = lax.axis_index("gx"), lax.axis_index("gy"), lax.axis_index("gz")
    y, c = gx // 2, gx % 2
    l, x = gz // 4, gz % 4
    z = 4 * h + l

    def dev(y_=y, c_=c, z_=z, x_=x):
        return {"gx": 2 * y_ + c_, "gy": z_ // 4, "gz": 4 * (z_ % 4) + x_}

    def remote(src, dst, s, r, to):
        return pltpu.make_async_remote_copy(
            src_ref=src, dst_ref=dst, send_sem=s, recv_sem=r,
            device_id=to, device_id_type=pl.DeviceIdType.MESH)

    x_up, x_dn, x_far = (x + 1) % 4, (x + 3) % 4, (x + 2) % 4
    y_up, y_dn, y_far = (y + 1) % 4, (y + 3) % 4, (y + 2) % 4
    z_up, z_dn = (z + 1) % RING, (z + RING - 1) % RING
    z_up4, z_dn4 = (z + 4) % RING, (z + RING - 4) % RING
    near = [dev(x_=x_up), dev(x_=x_dn), dev(y_=y_up), dev(y_=y_dn), dev(y_=y_far), dev(c_=1 - c),
            dev(z_=z_up), dev(z_=z_dn), dev(z_=z_up4), dev(z_=z_dn4)]
    near += [dev(z_=4 * h + (l + i) % 4) for i in (1, 2, 3)]

    barrier = pltpu.get_barrier_semaphore()
    for to in near:
        pl.semaphore_signal(barrier, inc=1, device_id=to, device_id_type=pl.DeviceIdType.MESH)
    own_b = pltpu.make_async_copy(b_ref, b_all.at[x], loc.at[0])
    own_b.start()
    state = [pltpu.make_async_copy(src, dst, loc.at[2 + i])
             for i, (src, dst) in enumerate([(w_ref, w_own), (m1_ref, m1_own), (m2_ref, m2_own)])]
    for copy in state:
        copy.start()
    pl.semaphore_wait(barrier, len(near))

    mine_at = pl.multiple_of(c * HALF, 128)

    def own(k):
        return a_ref.at[pl.ds(pl.multiple_of(k * ROWS, 16), ROWS), :]

    def held(i, k, first=0, wide=HALF):
        return at_all.at[i, k, :, pl.ds(pl.multiple_of(mine_at + first, 128), wide)]

    def scatter(dk, stays):
        k = (y + dk) % 4
        return remote(own(k), held(l, k) if stays else moved.at[y], sc_s.at[dk - 1], sc_r.at[dk - 1], dev(y_=k))

    def z_move(i, src, p):
        return remote(src, held(l, y), zm_s.at[i], zm_r.at[l], dev(z_=4 * h + p))

    stay = pltpu.make_async_copy(own(y), held(l, y), loc.at[1])

    @pl.when(y == l)
    def _():
        stay.start()
        for dk in (1, 3, 2):
            scatter(dk, True).start()

    @pl.when(y != l)
    def _():
        z_move(0, own(y), y).start()
        for dk in (1, 3, 2):
            scatter(dk, False).start()

    def b_move(q, half, up, slot):
        piece = pl.ds(half * (PART // 2), PART // 2)
        src = b_all.at[q, piece, :] if slot == 2 else b_ref.at[piece, :]
        return remote(src, b_all.at[q, piece, :], b_s.at[slot, up], b_r.at[slot, up],
                      dev(x_=x_up if up else x_dn))

    for slot in (0, 1):
        for up in (1, 0):
            b_move(x, slot if up else 1 - slot, up, slot).start()

    for dk in (1, 3, 2):
        p = (y + 4 - dk) % 4
        scatter(dk, False).wait_recv()

        @pl.when(p != l)
        def _():
            z_move(dk, moved.at[p], p).start()

    mirror = l // 2
    near_l = jnp.where(mirror == 1, 3 - l, l)
    order = [jnp.where(mirror == 1, 3 - i, i) for i in (near_l, 1 - near_l, 2, 3)]

    def hand_on(i, k):
        return remote(held(i, k), held(i, k), sib_s.at[i, k], sib_r.at[i, k], dev(c_=1 - c))

    def to_up(i):
        return remote(held(i, y), held(i, y), yp_s.at[i], yp_r.at[i], dev(y_=y_up))

    def to_dn(i):
        return remote(held(i, y), held(i, y), ym_s.at[i], ym_r.at[i], dev(y_=y_dn))

    def relay_up(i, k):
        piece = held(i, k, 0, HALF // 2)
        return remote(piece, piece, rp_s.at[i], rp_r.at[i], dev(y_=y_up))

    def relay_dn(i, k):
        piece = held(i, k, HALF // 2, HALF // 2)
        return remote(piece, piece, rm_s.at[i], rm_r.at[i], dev(y_=y_dn))

    def share(i):
        to_up(i).start()
        to_dn(i).start()
        hand_on(i, y).start()

    def relay(i):
        to_up(i).wait_recv()
        relay_up(i, y_dn).start()
        hand_on(i, y_dn).start()
        to_dn(i).wait_recv()
        relay_dn(i, y_up).start()
        hand_on(i, y_up).start()

    def far(i):
        relay_up(i, y_far).wait_recv()
        relay_dn(i, y_far).wait_recv()
        hand_on(i, y_far).start()

    @pl.when(y == l)
    def _():
        stay.wait()

    share(order[0])
    for up, q in ((1, x_dn), (0, x_up)):
        b_move(q, 1 - up, up, 0).wait_recv()
        b_move(q, 1 - up, up, 2).start()
    for n in (1, 2, 3):
        remote(moved.at[0], held(order[n], y), zm_s.at[0], zm_r.at[order[n]], dev(c_=1 - c)).wait_recv()
        share(order[n])
        relay(order[n - 1])
        if n >= 2:
            far(order[n - 2])
    relay(order[3])

    own_b.wait()
    for up in (1, 0):
        for slot in (1, 2):
            b_move(x, 0, up, slot).wait_recv()

    def product(n):
        i = order[n]
        for k in range(4):
            hand_on(i, k).wait_recv()

        @pl.loop(0, COLS // TILE)
        def _(j):
            cols = pl.ds(pl.multiple_of(j * TILE, TILE), TILE)
            total = jnp.dot(at_all[i].reshape(4 * ROWS, 2 * HALF), b_all[:, :, cols].reshape(2 * HALF, TILE),
                            preferred_element_type=F32)
            part[i, :, :, cols] = total.reshape(4, ROWS, TILE)

    def term(up, f, e):
        d = (z + e) % RING if up else (z + RING - e) % RING
        return part[d % 4, d // 4, :, pl.ds(f * WIDE, WIDE)]

    def hop(up, f, e):
        return remote(send.at[up, f, e - 1], recv.at[up, f, e - 1], rs_s.at[up, f, e - 1], rs_r.at[up, f, e - 1],
                      dev(z_=z_up if up else z_dn))

    def far_side(up, f):
        return up == (1 if f < CHUNKS // 2 else 0)

    def first_hop(up, f, e):
        send[up, f, e - 1] = term(up, f, e).astype(BF)
        hop(up, f, e).start()

    def next_hop(up, f, e):
        mine = term(up, f, e)
        hop(up, f, e + 1).wait_recv()
        send[up, f, e - 1] = (mine + recv[up, f, e].astype(F32)).astype(BF)
        hop(up, f, e).start()

    ways = [(1, 0), (0, CHUNKS // 2), (1, 1), (0, CHUNKS // 2 + 1)]
    late = [(1, CHUNKS // 2), (0, 0), (1, CHUNKS // 2 + 1), (0, 1)]

    product(0)
    for up, f in ways:
        first_hop(up, f, REACH)
    far(order[2])
    product(1)
    far(order[3])
    product(2)
    product(3)
    for (up, f), (up_, f_) in zip(late, ways):
        first_hop(up, f, REACH - 1)
        next_hop(up_, f_, REACH - 1)

    def ring_step(i, carry):
        for up, f in ways + late:
            next_hop(up, f, REACH - 2 - i)
        return carry

    lax.fori_loop(0, REACH - 2, ring_step, 0)

    def weights(f, k):
        return wn_ref.at[k, :, pl.ds(f * (WIDE), WIDE)]

    def weights_up(f):
        return remote(weights(f, h), weights(f, h), up_s.at[f], up_r.at[f], dev(z_=z_up4))

    def weights_dn(f):
        return remote(weights(f, h), weights(f, h), dn_s.at[f], dn_r.at[f], dev(z_=z_dn4))

    corr_one = 1.0 - beta_one**adam_step
    corr_two = 1.0 - beta_two**adam_step
    for copy in state:
        copy.wait()
    for f in [0, 2, 1, 3]:
        cols = pl.ds(f * WIDE, WIDE)
        grad = term(1, f, 0)
        for up in (1, 0):
            hop(up, f, 1).wait_recv()
        grad = grad + recv[1, f, 0].astype(F32) + recv[0, f, 0].astype(F32)
        first_next = beta_one * m1_own[:, cols] + (1.0 - beta_one) * grad
        second_next = beta_two * m2_own[:, cols] + (1.0 - beta_two) * grad * grad
        grad_ref[:, cols] = grad
        wide = w_own[:, cols].astype(F32)
        update = (first_next / corr_one / (jnp.sqrt(second_next / corr_two) + epsilon)
                  + decay_rate * wide)
        wn_ref[h, :, cols] = (wide - learn_rate * update).astype(BF)
        weights_up(f).start()
        weights_dn(f).start()

    h_dn, h_up, h_far = (h + 3) % 4, (h + 1) % 4, (h + 2) % 4

    def pass_up(f, k):
        return remote(weights(f, k), weights(f, k), fw_s.at[f], fw_r.at[f], dev(z_=z_up4))

    def pass_dn(f, k):
        return remote(weights(f, k), weights(f, k), fw_s.at[f], fw_r.at[f], dev(z_=z_dn4))

    for f in [0, 2, 1, 3]:
        if f < CHUNKS // 2:
            weights_up(f).wait_recv()
            pass_up(f, h_dn).start()
        else:
            weights_dn(f).wait_recv()
            pass_dn(f, h_up).start()
    for f in range(CHUNKS):
        if f < CHUNKS // 2:
            weights_dn(f).wait_recv()
        else:
            weights_up(f).wait_recv()
        pass_up(f, h_far).wait_recv()

    for slot in (0, 1, 2):
        for up in (1, 0):
            b_move(x, 0, up, slot).wait_send()
    for dk in (1, 2, 3):
        scatter(dk, False).wait_send()

        @pl.when((y + 4 - dk) % 4 != l)
        def _():
            z_move(dk, moved.at[0], l).wait_send()

    @pl.when(y != l)
    def _():
        z_move(0, own(y), l).wait_send()
    for i in range(4):
        to_up(i).wait_send()
        to_dn(i).wait_send()
        relay_up(i, 0).wait_send()
        relay_dn(i, 0).wait_send()
        for k in range(4):
            hand_on(i, k).wait_send()
    for f in range(CHUNKS):
        weights_up(f).wait_send()
        weights_dn(f).wait_send()
        pass_up(f, 0).wait_send()

    for up, f in ways:
        hop(up, f, REACH).wait_send()

    def drain(i, carry):
        for up, f in ways + late:
            hop(up, f, i + 1).wait_send()
        return carry

    lax.fori_loop(0, REACH - 1, drain, 0)


def body(inputs, out_grads, weights, first_moment, second_moment):
    vmem = pl.BlockSpec(memory_space=pltpu.VMEM)
    dma = pltpu.SemaphoreType.DMA
    own = first_moment.shape
    grad, weight_next = pl.pallas_call(
        kernel,
        name="adam_grad",
        out_shape=(jax.ShapeDtypeStruct(own, F32),
                   jax.ShapeDtypeStruct((4, ROWS, COLS), BF)),
        in_specs=[pl.BlockSpec(memory_space=pltpu.HBM)] * 5,
        out_specs=(vmem,) * 2,
        scratch_shapes=[
            pltpu.VMEM((4, ROWS, HALF), BF),
            pltpu.VMEM((4, 4, ROWS, 2 * HALF), BF),
            pltpu.VMEM((4, PART, COLS), BF),
            pltpu.VMEM((4, 4, ROWS, COLS), F32),
            pltpu.VMEM((2, CHUNKS, REACH, ROWS, WIDE), BF),
            pltpu.VMEM((2, CHUNKS, REACH, ROWS, WIDE), BF),
            pltpu.VMEM((ROWS, COLS), BF),
            pltpu.VMEM((ROWS, COLS), F32),
            pltpu.VMEM((ROWS, COLS), F32),
            dma((3,)), dma((3,)), dma((4,)), dma((4,)), dma((5,)),
            dma((4,)), dma((4,)), dma((4,)), dma((4,)),
            dma((4,)), dma((4,)), dma((4,)), dma((4,)),
            dma((4, 4)), dma((4, 4)),
            dma((3, 2)), dma((3, 2)),
            dma((2, CHUNKS, REACH)), dma((2, CHUNKS, REACH)),
            dma((CHUNKS,)), dma((CHUNKS,)), dma((CHUNKS,)), dma((CHUNKS,)),
            dma((CHUNKS,)), dma((CHUNKS,)),
        ],
        compiler_params=pltpu.CompilerParams(
            collective_id=0, has_side_effects=True, vmem_limit_bytes=60 * 2**20),
        cost_estimate=pl.CostEstimate(flops=5_700_000_000, bytes_accessed=6_000_000, transcendentals=0),
    )(inputs.T, out_grads, weights, first_moment, second_moment)
    first_next = beta_one * first_moment + (1.0 - beta_one) * grad
    second_next = beta_two * second_moment + (1.0 - beta_two) * grad * grad
    return first_next, second_next, weight_next.reshape(4 * ROWS, COLS)


def solution(mesh):
    in_specs = (
        P(("gy", "gx"), "gz"),
        P(("gy", "gz"), "gx"),
        P(("gz", "gy"), "gx"),
        P(("gz", "gy"), "gx"),
        P(("gz", "gy"), "gx"),
    )
    out_specs = (P(("gz", "gy"), "gx"), P(("gz", "gy"), "gx"), P("gz", "gx"))
    return jax.shard_map(body, mesh=mesh, in_specs=in_specs, out_specs=out_specs, check_vma=False)
```

```python
import functools
import jax
import jax.numpy as jnp
from jax import lax
from jax.experimental import pallas as pl
from jax.experimental.pallas import tpu as pltpu
from jax.sharding import PartitionSpec as P

beta_one = 0.9
beta_two = 0.95
adam_step = 10.0
learn_rate = 0.01
decay_rate = 0.1
epsilon = 1e-08

BF = jnp.bfloat16
F32 = jnp.float32

RING = 16
ROWS = 112
PART = 384
COLS = 1024
CHUNKS = 4
WIDE = COLS // CHUNKS
REACH = 8
TILE = 512


def kernel(a_ref, b_ref, w_ref, m1_ref, m2_ref, grad_ref, wn_ref,
           moved, at_all, b_all, part, recv, send, w_own, m1_own, m2_own,
           sc_s, sc_r, zm_s, zm_r, loc, stay_s, up_y, dn_y, nb_r, rl_s, rl_r,
           sib_s, sib_r, b_s, b_r, rs_s, rs_r, up_s, dn_s, up_r, dn_r, fw_s, fw_r):
    gx, h, gz = lax.axis_index("gx"), lax.axis_index("gy"), lax.axis_index("gz")
    y, c = gx // 2, gx % 2
    l, x = gz // 4, gz % 4
    z = 4 * h + l

    def dev(y_=y, c_=c, z_=z, x_=x):
        return {"gx": 2 * y_ + c_, "gy": z_ // 4, "gz": 4 * (z_ % 4) + x_}

    def remote(src, dst, s, r, to):
        return pltpu.make_async_remote_copy(
            src_ref=src, dst_ref=dst, send_sem=s, recv_sem=r,
            device_id=to, device_id_type=pl.DeviceIdType.MESH)

    x_up, x_dn = (x + 1) % 4, (x + 3) % 4
    y_up, y_dn, y_far = (y + 1) % 4, (y + 3) % 4, (y + 2) % 4
    z_up, z_dn = (z + 1) % RING, (z + RING - 1) % RING
    z_up4, z_dn4 = (z + 4) % RING, (z + RING - 4) % RING
    near = [dev(x_=x_up), dev(x_=x_dn), dev(y_=y_up), dev(y_=y_dn), dev(y_=y_far), dev(c_=1 - c),
            dev(z_=z_up), dev(z_=z_dn), dev(z_=z_up4), dev(z_=z_dn4)]
    near += [dev(z_=4 * h + (l + i) % 4) for i in (1, 2, 3)]

    barrier = pltpu.get_barrier_semaphore()
    for to in near:
        pl.semaphore_signal(barrier, inc=1, device_id=to, device_id_type=pl.DeviceIdType.MESH)
    own_b = pltpu.make_async_copy(b_ref, b_all.at[x], loc.at[0])
    own_b.start()
    state = [pltpu.make_async_copy(src, dst, loc.at[1 + i])
             for i, (src, dst) in enumerate([(w_ref, w_own), (m1_ref, m1_own), (m2_ref, m2_own)])]
    for copy in state:
        copy.start()
    pl.semaphore_wait(barrier, len(near))

    def number(up, e):
        return 0 if e == REACH else RING - 1 if e == 0 else 1 + 2 * (REACH - 1 - e) + (0 if up else 1)

    def pick(i, values):
        return jnp.where(i == 0, values[0], jnp.where(i == 1, values[1], jnp.where(i == 2, values[2], values[3])))

    turn = (y + 4 - 2 * c) % 4
    owner = turn < 2
    upward = jnp.logical_or(turn == 1, turn == 2)
    side = turn % 2

    def lanes(q):
        return pl.ds(pl.multiple_of(q * PART, 128), PART)

    def piece(n, q):
        return at_all.at[n, :, lanes(q)]

    def source(off, p, j):
        k = ((4 * h + p + off + RING) % RING) // 4
        return a_ref.at[pl.ds(pl.multiple_of(k * ROWS, 16), ROWS), lanes(j)]

    home = [0, number(True, 4), number(False, 4), RING - 1]
    offsets = [pick((l + 4 - y) % 4, v) for v in ([8, -7, 6, 7], [4, 5, -6, -5], [-4, -3, 2, 3], [0, 1, -2, -1])]

    def scatter(i, j, stays):
        q = 2 * c + j
        return remote(source(offsets[i], y, j), piece(home[i], q) if stays else moved.at[y, i],
                      sc_s.at[i, j], sc_r.at[y, i], dev(y_=q))

    def stay(i):
        return pltpu.make_async_copy(source(offsets[i], y, side), piece(home[i], y), stay_s.at[i])

    for i in range(4):
        for j in range(2):
            @pl.when(jnp.logical_and(2 * c + j != y, y == l))
            def _():
                scatter(i, j, True).start()

            @pl.when(jnp.logical_and(2 * c + j != y, y != l))
            def _():
                scatter(i, j, False).start()

        @pl.when(jnp.logical_and(owner, y == l))
        def _():
            stay(i).start()

    rank = {(1, 7): 0, (0, 7): 0, (1, 6): 0, (0, 6): 1, (1, 5): 1, (0, 5): 1,
            (1, 3): 2, (0, 3): 2, (1, 2): 2, (0, 2): 3, (1, 1): 3, (0, 1): 3}

    def z_move(src, n, p):
        return remote(src, piece(n, y), zm_s.at[n], zm_r.at[n], dev(z_=4 * h + p))

    def scattered(p, i):
        return remote(moved.at[p, i], moved.at[p, i], sc_s.at[0, 0], sc_r.at[p, i], dev(c_=1 - c))

    def z_moves(*which):
        for up, e in which:
            n = number(up, e)
            p = (l + 8 - e) % 4 if up else (l + e) % 4

            @pl.when(jnp.logical_and(owner, p == y))
            def _():
                z_move(source(e if up else -e, p, side), n, p).start()

            @pl.when(jnp.logical_and(owner, p != y))
            def _():
                scattered(p, rank[up, e]).wait_recv()
                z_move(moved.at[p, rank[up, e]], n, p).start()

    def b_move(q, half, up, slot):
        piece = pl.ds(half * (PART // 2), PART // 2)
        src = b_all.at[q, piece, :] if slot == 2 else b_ref.at[piece, :]
        return remote(src, b_all.at[q, piece, :], b_s.at[slot, up], b_r.at[slot, up],
                      dev(x_=x_up if up else x_dn))

    for slot in (0, 1):
        for up in (1, 0):
            b_move(x, slot if up else 1 - slot, up, slot).start()

    def to_up(n):
        return remote(piece(n, y), piece(n, y), up_y.at[n], nb_r.at[n], dev(y_=y_up))

    def to_dn(n):
        return remote(piece(n, y), piece(n, y), dn_y.at[n], nb_r.at[n], dev(y_=y_dn))

    def from_near(n):
        return piece(n, 2 * c + 1 - side)

    def pass_along(n):
        return remote(from_near(n), from_near(n), rl_s.at[n], rl_r.at[n], dev(y_=y_up if n % 2 else y_dn))

    def passes(n):
        return upward if n % 2 else jnp.logical_not(upward)

    def hand_on(n, j):
        return remote(piece(n, 2 * c + j), piece(n, 2 * c + j), sib_s.at[n, j], sib_r.at[n, j], dev(c_=1 - c))

    def share(*blocks):
        for n in blocks:
            if n in home:
                i = home.index(n)

                @pl.when(jnp.logical_and(owner, y == l))
                def _():
                    stay(i).wait()

                @pl.when(jnp.logical_and(owner, y != l))
                def _():
                    remote(moved.at[0, 0], piece(n, y), sc_s.at[0, 0], sc_r.at[l, i], dev(c_=1 - c)).wait_recv()
            else:
                @pl.when(owner)
                def _():
                    z_move(moved.at[0, 0], n, l).wait_recv()

            @pl.when(owner)
            def _():
                to_up(n).start()
                to_dn(n).start()
                hand_on(n, side).start()

    def relay(*blocks):
        for n in blocks:
            remote(from_near(n), from_near(n), up_y.at[n], nb_r.at[n], dev(c_=1 - c)).wait_recv()

            @pl.when(passes(n))
            def _():
                pass_along(n).start()
            hand_on(n, 1 - side).start()

    def far(*blocks):
        for n in blocks:
            @pl.when(jnp.logical_not(owner))
            def _():
                remote(moved.at[0, 0], piece(n, 2 * c + side), rl_s.at[n], rl_r.at[n], dev(c_=1 - c)).wait_recv()
                hand_on(n, side).start()

    def product(*blocks):
        for n in blocks:
            for j in range(2):
                remote(moved.at[0, 0], piece(n, 2 - 2 * c + j), sib_s.at[n, j], sib_r.at[n, j], dev(c_=1 - c)).wait_recv()

            @pl.loop(0, COLS // TILE)
            def _(j):
                cols = pl.ds(pl.multiple_of(j * TILE, TILE), TILE)
                part[n, :, cols] = jnp.dot(at_all[n], b_all[:, :, cols].reshape(4 * PART, TILE),
                                           preferred_element_type=F32)

    def term(up, f, e):
        return part[number(up, e), :, pl.ds(f * WIDE, WIDE)]

    def hop(up, f, e):
        return remote(send.at[up, f, e - 1], recv.at[up, f, e - 1], rs_s.at[up, f, e - 1], rs_r.at[up, f, e - 1],
                      dev(z_=z_up if up else z_dn))

    def far_side(up, f):
        return up == (1 if f < CHUNKS // 2 else 0)

    def first_hop(up, f, e):
        send[up, f, e - 1] = term(up, f, e).astype(BF)
        hop(up, f, e).start()

    def next_hop(up, f, e):
        mine = term(up, f, e)
        hop(up, f, e + 1).wait_recv()
        send[up, f, e - 1] = (mine + recv[up, f, e].astype(F32)).astype(BF)
        hop(up, f, e).start()

    def hops(e):
        for f in (0, 2, 1, 3):
            for up in ((1, 0) if f < CHUNKS // 2 else (0, 1)):
                if e < REACH - 1 or (e == REACH - 1 and far_side(up, f)):
                    next_hop(up, f, e)
                elif e == REACH - 1 or far_side(up, f):
                    first_hop(up, f, e)

    z_moves((1, 7), (0, 7))
    share(0)
    z_moves((1, 6), (0, 6), (1, 5), (0, 5))
    relay(0)
    share(1, 2)
    for up, q in ((1, x_dn), (0, x_up)):
        b_move(q, 1 - up, up, 0).wait_recv()
        b_move(q, 1 - up, up, 2).start()
    far(0)
    relay(1, 2)
    share(3, 4)
    z_moves((1, 3), (0, 3))
    far(1, 2)
    relay(3, 4)
    share(5, 6)
    z_moves((1, 2), (0, 2), (1, 1), (0, 1))
    far(3, 4)
    relay(5, 6)
    share(7, 8)

    own_b.wait()
    for up in (1, 0):
        for slot in (1, 2):
            b_move(x, 0, up, slot).wait_recv()

    product(0)
    hops(8)
    far(5, 6)
    relay(7, 8)
    share(9, 10)
    product(1, 2)
    hops(7)
    far(7, 8)
    relay(9, 10)
    share(11, 12)
    product(3, 4)
    hops(6)
    far(9, 10)
    relay(11, 12)
    share(13, 14)
    product(5, 6)
    hops(5)
    far(11, 12)
    relay(13, 14)
    share(15)
    product(7, 8)
    hops(4)
    far(13, 14)
    relay(15)
    product(9, 10)
    hops(3)
    far(15)
    product(11, 12)
    hops(2)
    product(13, 14)
    hops(1)
    product(15)

    def weights(f, k):
        return wn_ref.at[k, :, pl.ds(f * (WIDE), WIDE)]

    def weights_up(f):
        return remote(weights(f, h), weights(f, h), up_s.at[f], up_r.at[f], dev(z_=z_up4))

    def weights_dn(f):
        return remote(weights(f, h), weights(f, h), dn_s.at[f], dn_r.at[f], dev(z_=z_dn4))

    corr_one = 1.0 - beta_one**adam_step
    corr_two = 1.0 - beta_two**adam_step
    for copy in state:
        copy.wait()
    for f in [0, 2, 1, 3]:
        cols = pl.ds(f * WIDE, WIDE)
        grad = term(1, f, 0)
        for up in (1, 0):
            hop(up, f, 1).wait_recv()
        grad = grad + recv[1, f, 0].astype(F32) + recv[0, f, 0].astype(F32)
        first_next = beta_one * m1_own[:, cols] + (1.0 - beta_one) * grad
        second_next = beta_two * m2_own[:, cols] + (1.0 - beta_two) * grad * grad
        grad_ref[:, cols] = grad
        wide = w_own[:, cols].astype(F32)
        update = (first_next / corr_one / (jnp.sqrt(second_next / corr_two) + epsilon)
                  + decay_rate * wide)
        wn_ref[h, :, cols] = (wide - learn_rate * update).astype(BF)
        weights_up(f).start()
        weights_dn(f).start()

    h_dn, h_up, h_far = (h + 3) % 4, (h + 1) % 4, (h + 2) % 4

    def pass_up(f, k):
        return remote(weights(f, k), weights(f, k), fw_s.at[f], fw_r.at[f], dev(z_=z_up4))

    def pass_dn(f, k):
        return remote(weights(f, k), weights(f, k), fw_s.at[f], fw_r.at[f], dev(z_=z_dn4))

    for f in [0, 2, 1, 3]:
        if f < CHUNKS // 2:
            weights_up(f).wait_recv()
            pass_up(f, h_dn).start()
        else:
            weights_dn(f).wait_recv()
            pass_dn(f, h_up).start()
    for f in range(CHUNKS):
        if f < CHUNKS // 2:
            weights_dn(f).wait_recv()
        else:
            weights_up(f).wait_recv()
        pass_up(f, h_far).wait_recv()

    for slot in (0, 1, 2):
        for up in (1, 0):
            b_move(x, 0, up, slot).wait_send()
    for i in range(4):
        for j in range(2):
            @pl.when(2 * c + j != y)
            def _():
                scatter(i, j, False).wait_send()

    @pl.when(owner)
    def _():
        for n in range(RING):
            if n not in home:
                z_move(moved.at[0, 0], n, l).wait_send()
    for n in range(RING):
        @pl.when(owner)
        def _():
            to_up(n).wait_send()
            to_dn(n).wait_send()

        @pl.when(passes(n))
        def _():
            pass_along(n).wait_send()
        for j in range(2):
            hand_on(n, j).wait_send()
    for f in range(CHUNKS):
        weights_up(f).wait_send()
        weights_dn(f).wait_send()
        pass_up(f, 0).wait_send()

    for e in range(1, REACH + 1):
        for f in range(CHUNKS):
            for up in (1, 0):
                if e < REACH or far_side(up, f):
                    hop(up, f, e).wait_send()


def body(inputs, out_grads, weights, first_moment, second_moment):
    vmem = pl.BlockSpec(memory_space=pltpu.VMEM)
    dma = pltpu.SemaphoreType.DMA
    own = first_moment.shape
    grad, weight_next = pl.pallas_call(
        kernel,
        name="adam_grad",
        out_shape=(jax.ShapeDtypeStruct(own, F32),
                   jax.ShapeDtypeStruct((4, ROWS, COLS), BF)),
        in_specs=[pl.BlockSpec(memory_space=pltpu.HBM)] * 5,
        out_specs=(vmem,) * 2,
        scratch_shapes=[
            pltpu.VMEM((4, 4, ROWS, PART), BF),
            pltpu.VMEM((RING, ROWS, 4 * PART), BF),
            pltpu.VMEM((4, PART, COLS), BF),
            pltpu.VMEM((RING, ROWS, COLS), F32),
            pltpu.VMEM((2, CHUNKS, REACH, ROWS, WIDE), BF),
            pltpu.VMEM((2, CHUNKS, REACH, ROWS, WIDE), BF),
            pltpu.VMEM((ROWS, COLS), BF),
            pltpu.VMEM((ROWS, COLS), F32),
            pltpu.VMEM((ROWS, COLS), F32),
            dma((4, 2)), dma((4, 4)), dma((RING,)), dma((RING,)), dma((4,)), dma((4,)),
            dma((RING,)), dma((RING,)), dma((RING,)), dma((RING,)), dma((RING,)),
            dma((RING, 2)), dma((RING, 2)),
            dma((3, 2)), dma((3, 2)),
            dma((2, CHUNKS, REACH)), dma((2, CHUNKS, REACH)),
            dma((CHUNKS,)), dma((CHUNKS,)), dma((CHUNKS,)), dma((CHUNKS,)),
            dma((CHUNKS,)), dma((CHUNKS,)),
        ],
        compiler_params=pltpu.CompilerParams(
            collective_id=0, has_side_effects=True, vmem_limit_bytes=60 * 2**20),
        cost_estimate=pl.CostEstimate(flops=5_700_000_000, bytes_accessed=6_000_000, transcendentals=0),
    )(inputs.T, out_grads, weights, first_moment, second_moment)
    first_next = beta_one * first_moment + (1.0 - beta_one) * grad
    second_next = beta_two * second_moment + (1.0 - beta_two) * grad * grad
    return first_next, second_next, weight_next.reshape(4 * ROWS, COLS)


def solution(mesh):
    in_specs = (
        P(("gy", "gx"), "gz"),
        P(("gy", "gz"), "gx"),
        P(("gz", "gy"), "gx"),
        P(("gz", "gy"), "gx"),
        P(("gz", "gy"), "gx"),
    )
    out_specs = (P(("gz", "gy"), "gx"), P(("gz", "gy"), "gx"), P("gz", "gx"))
    return jax.shard_map(body, mesh=mesh, in_specs=in_specs, out_specs=out_specs, check_vma=False)
```

```python
import functools
import jax
import jax.numpy as jnp
from jax import lax
from jax.experimental import pallas as pl
from jax.experimental.pallas import tpu as pltpu
from jax.sharding import PartitionSpec as P

beta_one = 0.9
beta_two = 0.95
adam_step = 10.0
learn_rate = 0.01
decay_rate = 0.1
epsilon = 1e-08

BF = jnp.bfloat16
F32 = jnp.float32

RING = 16
ROWS = 112
PART = 384
COLS = 1024
CHUNKS = 4
WIDE = COLS // CHUNKS
REACH = 8
TILE = 512


def kernel(a_ref, b_ref, w_ref, m1_ref, m2_ref, grad_ref, wn_ref,
           moved, at_all, b_all, part, recv, send, w_own, m1_own, m2_own,
           sc_s, sc_r, zm_s, zm_r, loc, stay_s, up_y, dn_y, nb_r, rl_s, rl_r,
           sib_s, sib_r, b_s, b_r, rs_s, rs_r, up_s, dn_s, up_r, dn_r, fw_s, fw_r):
    gx, h, gz = lax.axis_index("gx"), lax.axis_index("gy"), lax.axis_index("gz")
    y, c = gx // 2, gx % 2
    l, x = gz // 4, gz % 4
    z = 4 * h + l

    def dev(y_=y, c_=c, z_=z, x_=x):
        return {"gx": 2 * y_ + c_, "gy": z_ // 4, "gz": 4 * (z_ % 4) + x_}

    def remote(src, dst, s, r, to):
        return pltpu.make_async_remote_copy(
            src_ref=src, dst_ref=dst, send_sem=s, recv_sem=r,
            device_id=to, device_id_type=pl.DeviceIdType.MESH)

    x_up, x_dn = (x + 1) % 4, (x + 3) % 4
    y_up, y_dn, y_far = (y + 1) % 4, (y + 3) % 4, (y + 2) % 4
    z_up, z_dn = (z + 1) % RING, (z + RING - 1) % RING
    z_up4, z_dn4 = (z + 4) % RING, (z + RING - 4) % RING
    near = [dev(x_=x_up), dev(x_=x_dn), dev(y_=y_up), dev(y_=y_dn), dev(y_=y_far), dev(c_=1 - c),
            dev(z_=z_up), dev(z_=z_dn), dev(z_=z_up4), dev(z_=z_dn4)]
    near += [dev(z_=4 * h + (l + i) % 4) for i in (1, 2, 3)]

    barrier = pltpu.get_barrier_semaphore()
    for to in near:
        pl.semaphore_signal(barrier, inc=1, device_id=to, device_id_type=pl.DeviceIdType.MESH)
    own_b = pltpu.make_async_copy(b_ref, b_all.at[x], loc.at[0])
    own_b.start()
    state = [pltpu.make_async_copy(src, dst, loc.at[1 + i])
             for i, (src, dst) in enumerate([(w_ref, w_own), (m1_ref, m1_own), (m2_ref, m2_own)])]
    for copy in state:
        copy.start()
    pl.semaphore_wait(barrier, len(near))

    def number(up, e):
        return 0 if e == REACH else RING - 1 if e == 0 else 1 + 2 * (REACH - 1 - e) + (0 if up else 1)

    def pick(i, values):
        return jnp.where(i == 0, values[0], jnp.where(i == 1, values[1], jnp.where(i == 2, values[2], values[3])))

    turn = (y + 4 - 2 * c) % 4
    owner = turn < 2
    upward = jnp.logical_or(turn == 1, turn == 2)
    side = turn % 2

    def lanes(q):
        return pl.ds(pl.multiple_of(q * PART, 128), PART)

    def piece(n, q):
        return at_all.at[n, :, lanes(q)]

    def source(off, p, j):
        k = ((4 * h + p + off + RING) % RING) // 4
        return a_ref.at[pl.ds(pl.multiple_of(k * ROWS, 16), ROWS), lanes(j)]

    home = [0, number(True, 4), number(False, 4), RING - 1]
    offsets = [pick((l + 4 - y) % 4, v) for v in ([8, -7, 6, 7], [4, 5, -6, -5], [-4, -3, 2, 3], [0, 1, -2, -1])]

    def scatter(i, j, stays):
        q = 2 * c + j
        return remote(source(offsets[i], y, j), piece(home[i], q) if stays else moved.at[y, i],
                      sc_s.at[i, j], sc_r.at[y, i], dev(y_=q))

    def stay(i):
        return pltpu.make_async_copy(source(offsets[i], y, side), piece(home[i], y), stay_s.at[i])

    for i in range(4):
        for j in range(2):
            @pl.when(jnp.logical_and(2 * c + j != y, y == l))
            def _():
                scatter(i, j, True).start()

            @pl.when(jnp.logical_and(2 * c + j != y, y != l))
            def _():
                scatter(i, j, False).start()

        @pl.when(jnp.logical_and(owner, y == l))
        def _():
            stay(i).start()

    rank = {(1, 7): 0, (0, 7): 0, (1, 6): 0, (0, 6): 1, (1, 5): 1, (0, 5): 1,
            (1, 3): 2, (0, 3): 2, (1, 2): 2, (0, 2): 3, (1, 1): 3, (0, 1): 3}

    def z_move(src, n, p):
        return remote(src, piece(n, y), zm_s.at[n], zm_r.at[n], dev(z_=4 * h + p))

    def scattered(p, i):
        return remote(moved.at[p, i], moved.at[p, i], sc_s.at[0, 0], sc_r.at[p, i], dev(c_=1 - c))

    def z_moves(*which):
        for up, e in which:
            n = number(up, e)
            p = (l + 8 - e) % 4 if up else (l + e) % 4

            @pl.when(jnp.logical_and(owner, p == y))
            def _():
                z_move(source(e if up else -e, p, side), n, p).start()

            @pl.when(jnp.logical_and(owner, p != y))
            def _():
                scattered(p, rank[up, e]).wait_recv()
                z_move(moved.at[p, rank[up, e]], n, p).start()

    def b_move(q, half, up, slot):
        piece = pl.ds(half * (PART // 2), PART // 2)
        src = b_all.at[q, piece, :] if slot == 2 else b_ref.at[piece, :]
        return remote(src, b_all.at[q, piece, :], b_s.at[slot, up], b_r.at[slot, up],
                      dev(x_=x_up if up else x_dn))

    for slot in (0, 1):
        for up in (1, 0):
            b_move(x, slot if up else 1 - slot, up, slot).start()

    def to_up(n):
        return remote(piece(n, y), piece(n, y), up_y.at[n], nb_r.at[n], dev(y_=y_up))

    def to_dn(n):
        return remote(piece(n, y), piece(n, y), dn_y.at[n], nb_r.at[n], dev(y_=y_dn))

    def from_near(n):
        return piece(n, 2 * c + 1 - side)

    def pass_along(n):
        return remote(from_near(n), from_near(n), rl_s.at[n], rl_r.at[n], dev(y_=y_up if n % 2 else y_dn))

    def passes(n):
        return upward if n % 2 else jnp.logical_not(upward)

    def hand_on(n, j):
        return remote(piece(n, 2 * c + j), piece(n, 2 * c + j), sib_s.at[n, j], sib_r.at[n, j], dev(c_=1 - c))

    def share(*blocks):
        for n in blocks:
            if n in home:
                i = home.index(n)

                @pl.when(jnp.logical_and(owner, y == l))
                def _():
                    stay(i).wait()

                @pl.when(jnp.logical_and(owner, y != l))
                def _():
                    remote(moved.at[0, 0], piece(n, y), sc_s.at[0, 0], sc_r.at[l, i], dev(c_=1 - c)).wait_recv()
            else:
                @pl.when(owner)
                def _():
                    z_move(moved.at[0, 0], n, l).wait_recv()

            @pl.when(owner)
            def _():
                to_up(n).start()
                to_dn(n).start()
                hand_on(n, side).start()

    def relay(*blocks):
        for n in blocks:
            remote(from_near(n), from_near(n), up_y.at[n], nb_r.at[n], dev(c_=1 - c)).wait_recv()

            @pl.when(passes(n))
            def _():
                pass_along(n).start()
            hand_on(n, 1 - side).start()

    def far(*blocks):
        for n in blocks:
            @pl.when(jnp.logical_not(owner))
            def _():
                remote(moved.at[0, 0], piece(n, 2 * c + side), rl_s.at[n], rl_r.at[n], dev(c_=1 - c)).wait_recv()
                hand_on(n, side).start()

    def product(*blocks):
        for n in blocks:
            for j in range(2):
                remote(moved.at[0, 0], piece(n, 2 - 2 * c + j), sib_s.at[n, j], sib_r.at[n, j], dev(c_=1 - c)).wait_recv()

            @pl.loop(0, COLS // TILE)
            def _(j):
                cols = pl.ds(pl.multiple_of(j * TILE, TILE), TILE)
                part[n, :, cols] = jnp.dot(at_all[n], b_all[:, :, cols].reshape(4 * PART, TILE),
                                           preferred_element_type=F32)

    def term(up, f, e):
        return part[number(up, e), :, pl.ds(f * WIDE, WIDE)]

    def hop(up, f, e):
        return remote(send.at[up, f, e - 1], recv.at[up, f, e - 1], rs_s.at[up, f, e - 1], rs_r.at[up, f, e - 1],
                      dev(z_=z_up if up else z_dn))

    def far_side(up, f):
        return up == (1 if f < CHUNKS // 2 else 0)

    def first_hop(up, f, e):
        send[up, f, e - 1] = term(up, f, e).astype(BF)
        hop(up, f, e).start()

    def next_hop(up, f, e):
        mine = term(up, f, e)
        hop(up, f, e + 1).wait_recv()
        send[up, f, e - 1] = (mine + recv[up, f, e].astype(F32)).astype(BF)
        hop(up, f, e).start()

    def hops(e):
        for f in (0, 2, 1, 3):
            for up in ((1, 0) if f < CHUNKS // 2 else (0, 1)):
                if e < REACH - 1 or (e == REACH - 1 and far_side(up, f)):
                    next_hop(up, f, e)
                elif e == REACH - 1 or far_side(up, f):
                    first_hop(up, f, e)

    z_moves((1, 7), (0, 7))
    share(0)
    z_moves((1, 6), (0, 6), (1, 5), (0, 5))
    share(1, 2)
    relay(0)
    for up, q in ((1, x_dn), (0, x_up)):
        b_move(q, 1 - up, up, 0).wait_recv()
        b_move(q, 1 - up, up, 2).start()
    share(3, 4)
    relay(1, 2)
    far(0)
    z_moves((1, 3), (0, 3), (1, 2), (0, 2), (1, 1), (0, 1))
    share(5, 6)
    relay(3, 4)
    far(1, 2)
    share(7, 8)
    relay(5, 6)
    far(3, 4)
    share(9, 10)
    relay(7, 8)
    far(5, 6)

    own_b.wait()
    for up in (1, 0):
        for slot in (1, 2):
            b_move(x, 0, up, slot).wait_recv()

    product(0)
    hops(8)
    share(11, 12)
    relay(9, 10)
    far(7, 8)
    product(1, 2)
    hops(7)
    share(13, 14, 15)
    relay(11, 12)
    far(9, 10)
    product(3, 4)
    hops(6)
    relay(13, 14, 15)
    far(11, 12)
    product(5, 6)
    hops(5)
    far(13, 14, 15)
    product(7, 8)
    hops(4)
    product(9, 10)
    hops(3)
    product(11, 12)
    hops(2)
    product(13, 14)
    hops(1)
    product(15)

    def weights(f, k):
        return wn_ref.at[k, :, pl.ds(f * (WIDE), WIDE)]

    def weights_up(f):
        return remote(weights(f, h), weights(f, h), up_s.at[f], up_r.at[f], dev(z_=z_up4))

    def weights_dn(f):
        return remote(weights(f, h), weights(f, h), dn_s.at[f], dn_r.at[f], dev(z_=z_dn4))

    corr_one = 1.0 - beta_one**adam_step
    corr_two = 1.0 - beta_two**adam_step
    for copy in state:
        copy.wait()
    for f in [0, 2, 1, 3]:
        cols = pl.ds(f * WIDE, WIDE)
        grad = term(1, f, 0)
        for up in (1, 0):
            hop(up, f, 1).wait_recv()
        grad = grad + recv[1, f, 0].astype(F32) + recv[0, f, 0].astype(F32)
        first_next = beta_one * m1_own[:, cols] + (1.0 - beta_one) * grad
        second_next = beta_two * m2_own[:, cols] + (1.0 - beta_two) * grad * grad
        grad_ref[:, cols] = grad
        wide = w_own[:, cols].astype(F32)
        update = (first_next / corr_one / (jnp.sqrt(second_next / corr_two) + epsilon)
                  + decay_rate * wide)
        wn_ref[h, :, cols] = (wide - learn_rate * update).astype(BF)
        (weights_up if f < CHUNKS // 2 else weights_dn)(f).start()
    for f in [0, 2, 1, 3]:
        (weights_dn if f < CHUNKS // 2 else weights_up)(f).start()

    h_dn, h_up, h_far = (h + 3) % 4, (h + 1) % 4, (h + 2) % 4

    def pass_up(f, k):
        return remote(weights(f, k), weights(f, k), fw_s.at[f], fw_r.at[f], dev(z_=z_up4))

    def pass_dn(f, k):
        return remote(weights(f, k), weights(f, k), fw_s.at[f], fw_r.at[f], dev(z_=z_dn4))

    for f in [0, 2, 1, 3]:
        if f < CHUNKS // 2:
            weights_up(f).wait_recv()
            pass_up(f, h_dn).start()
        else:
            weights_dn(f).wait_recv()
            pass_dn(f, h_up).start()
    for f in range(CHUNKS):
        if f < CHUNKS // 2:
            weights_dn(f).wait_recv()
        else:
            weights_up(f).wait_recv()
        pass_up(f, h_far).wait_recv()

    for slot in (0, 1, 2):
        for up in (1, 0):
            b_move(x, 0, up, slot).wait_send()
    for i in range(4):
        for j in range(2):
            @pl.when(2 * c + j != y)
            def _():
                scatter(i, j, False).wait_send()

    @pl.when(owner)
    def _():
        for n in range(RING):
            if n not in home:
                z_move(moved.at[0, 0], n, l).wait_send()
    for n in range(RING):
        @pl.when(owner)
        def _():
            to_up(n).wait_send()
            to_dn(n).wait_send()

        @pl.when(passes(n))
        def _():
            pass_along(n).wait_send()
        for j in range(2):
            hand_on(n, j).wait_send()
    for f in range(CHUNKS):
        weights_up(f).wait_send()
        weights_dn(f).wait_send()
        pass_up(f, 0).wait_send()

    for e in range(1, REACH + 1):
        for f in range(CHUNKS):
            for up in (1, 0):
                if e < REACH or far_side(up, f):
                    hop(up, f, e).wait_send()


def body(inputs, out_grads, weights, first_moment, second_moment):
    vmem = pl.BlockSpec(memory_space=pltpu.VMEM)
    dma = pltpu.SemaphoreType.DMA
    own = first_moment.shape
    grad, weight_next = pl.pallas_call(
        kernel,
        name="adam_grad",
        out_shape=(jax.ShapeDtypeStruct(own, F32),
                   jax.ShapeDtypeStruct((4, ROWS, COLS), BF)),
        in_specs=[pl.BlockSpec(memory_space=pltpu.HBM)] * 5,
        out_specs=(vmem,) * 2,
        scratch_shapes=[
            pltpu.VMEM((4, 4, ROWS, PART), BF),
            pltpu.VMEM((RING, ROWS, 4 * PART), BF),
            pltpu.VMEM((4, PART, COLS), BF),
            pltpu.VMEM((RING, ROWS, COLS), F32),
            pltpu.VMEM((2, CHUNKS, REACH, ROWS, WIDE), BF),
            pltpu.VMEM((2, CHUNKS, REACH, ROWS, WIDE), BF),
            pltpu.VMEM((ROWS, COLS), BF),
            pltpu.VMEM((ROWS, COLS), F32),
            pltpu.VMEM((ROWS, COLS), F32),
            dma((4, 2)), dma((4, 4)), dma((RING,)), dma((RING,)), dma((4,)), dma((4,)),
            dma((RING,)), dma((RING,)), dma((RING,)), dma((RING,)), dma((RING,)),
            dma((RING, 2)), dma((RING, 2)),
            dma((3, 2)), dma((3, 2)),
            dma((2, CHUNKS, REACH)), dma((2, CHUNKS, REACH)),
            dma((CHUNKS,)), dma((CHUNKS,)), dma((CHUNKS,)), dma((CHUNKS,)),
            dma((CHUNKS,)), dma((CHUNKS,)),
        ],
        compiler_params=pltpu.CompilerParams(
            collective_id=0, has_side_effects=True, vmem_limit_bytes=60 * 2**20),
        cost_estimate=pl.CostEstimate(flops=5_700_000_000, bytes_accessed=6_000_000, transcendentals=0),
    )(inputs.T, out_grads, weights, first_moment, second_moment)
    first_next = beta_one * first_moment + (1.0 - beta_one) * grad
    second_next = beta_two * second_moment + (1.0 - beta_two) * grad * grad
    return first_next, second_next, weight_next.reshape(4 * ROWS, COLS)


def solution(mesh):
    in_specs = (
        P(("gy", "gx"), "gz"),
        P(("gy", "gz"), "gx"),
        P(("gz", "gy"), "gx"),
        P(("gz", "gy"), "gx"),
        P(("gz", "gy"), "gx"),
    )
    out_specs = (P(("gz", "gy"), "gx"), P(("gz", "gy"), "gx"), P("gz", "gx"))
    return jax.shard_map(body, mesh=mesh, in_specs=in_specs, out_specs=out_specs, check_vma=False)
```

```python
import functools
import jax
import jax.numpy as jnp
from jax import lax
from jax.experimental import pallas as pl
from jax.experimental.pallas import tpu as pltpu
from jax.sharding import PartitionSpec as P

beta_one = 0.9
beta_two = 0.95
adam_step = 10.0
learn_rate = 0.01
decay_rate = 0.1
epsilon = 1e-08

BF = jnp.bfloat16
F32 = jnp.float32

RING = 16
ROWS = 112
PART = 384
COLS = 1024
CHUNKS = 4
WIDE = COLS // CHUNKS
REACH = 8
TILE = 1024


def kernel(a_ref, b_ref, w_ref, m1_ref, m2_ref, grad_ref, wn_ref,
           moved, at_all, b_all, part, recv, send, w_own, m1_own, m2_own,
           sc_s, sc_r, zm_s, zm_r, loc, stay_s, up_y, dn_y, nb_r, rl_s, rl_r,
           sib_s, sib_r, b_s, b_r, rs_s, rs_r, up_s, dn_s, up_r, dn_r, fw_s, fw_r):
    gx, h, gz = lax.axis_index("gx"), lax.axis_index("gy"), lax.axis_index("gz")
    y, c = gx // 2, gx % 2
    l, x = gz // 4, gz % 4
    z = 4 * h + l

    def dev(y_=y, c_=c, z_=z, x_=x):
        return {"gx": 2 * y_ + c_, "gy": z_ // 4, "gz": 4 * (z_ % 4) + x_}

    def remote(src, dst, s, r, to):
        return pltpu.make_async_remote_copy(
            src_ref=src, dst_ref=dst, send_sem=s, recv_sem=r,
            device_id=to, device_id_type=pl.DeviceIdType.MESH)

    x_up, x_dn = (x + 1) % 4, (x + 3) % 4
    y_up, y_dn, y_far = (y + 1) % 4, (y + 3) % 4, (y + 2) % 4
    z_up, z_dn = (z + 1) % RING, (z + RING - 1) % RING
    z_up4, z_dn4 = (z + 4) % RING, (z + RING - 4) % RING
    near = [dev(x_=x_up), dev(x_=x_dn), dev(y_=y_up), dev(y_=y_dn), dev(y_=y_far), dev(c_=1 - c),
            dev(z_=z_up), dev(z_=z_dn), dev(z_=z_up4), dev(z_=z_dn4)]
    near += [dev(z_=4 * h + (l + i) % 4) for i in (1, 2, 3)]

    barrier = pltpu.get_barrier_semaphore()
    for to in near:
        pl.semaphore_signal(barrier, inc=1, device_id=to, device_id_type=pl.DeviceIdType.MESH)
    own_b = pltpu.make_async_copy(b_ref, b_all.at[x], loc.at[0])
    own_b.start()
    state = [pltpu.make_async_copy(src, dst, loc.at[1 + i])
             for i, (src, dst) in enumerate([(w_ref, w_own), (m1_ref, m1_own), (m2_ref, m2_own)])]
    for copy in state:
        copy.start()
    pl.semaphore_wait(barrier, len(near))

    def b_move(q, half, up, slot):
        piece = pl.ds(half * (PART // 2), PART // 2)
        src = b_all.at[q, piece, :] if slot == 2 else b_ref.at[piece, :]
        return remote(src, b_all.at[q, piece, :], b_s.at[slot, up], b_r.at[slot, up],
                      dev(x_=x_up if up else x_dn))

    for slot in (0, 1):
        for up in (1, 0):
            b_move(x, slot if up else 1 - slot, up, slot).start()

    def number(up, e):
        return 0 if e == REACH else RING - 1 if e == 0 else 1 + 2 * (REACH - 1 - e) + (0 if up else 1)

    def pick(i, values):
        return jnp.where(i == 0, values[0], jnp.where(i == 1, values[1], jnp.where(i == 2, values[2], values[3])))

    turn = (y + 4 - 2 * c) % 4
    owner = turn < 2
    upward = jnp.logical_or(turn == 1, turn == 2)
    side = turn % 2

    def lanes(q):
        return pl.ds(pl.multiple_of(q * PART, 128), PART)

    def piece(n, q):
        return at_all.at[n, :, lanes(q)]

    def source(off, p, j):
        k = ((4 * h + p + off + RING) % RING) // 4
        return a_ref.at[pl.ds(pl.multiple_of(k * ROWS, 16), ROWS), lanes(j)]

    home = [0, number(True, 4), number(False, 4), RING - 1]
    offsets = [pick((l + 4 - y) % 4, v) for v in ([8, -7, 6, 7], [4, 5, -6, -5], [-4, -3, 2, 3], [0, 1, -2, -1])]

    def scatter(i, j, stays):
        q = 2 * c + j
        return remote(source(offsets[i], y, j), piece(home[i], q) if stays else moved.at[y, i],
                      sc_s.at[i, j], sc_r.at[y, i], dev(y_=q))

    def stay(i):
        return pltpu.make_async_copy(source(offsets[i], y, side), piece(home[i], y), stay_s.at[i])

    for i in range(4):
        for j in range(2):
            @pl.when(jnp.logical_and(2 * c + j != y, y == l))
            def _():
                scatter(i, j, True).start()

            @pl.when(jnp.logical_and(2 * c + j != y, y != l))
            def _():
                scatter(i, j, False).start()

        @pl.when(jnp.logical_and(owner, y == l))
        def _():
            stay(i).start()

    rank = {(1, 7): 0, (0, 7): 0, (1, 6): 0, (0, 6): 1, (1, 5): 1, (0, 5): 1,
            (1, 3): 2, (0, 3): 2, (1, 2): 2, (0, 2): 3, (1, 1): 3, (0, 1): 3}

    def z_move(src, n, p):
        return remote(src, piece(n, y), zm_s.at[n], zm_r.at[n], dev(z_=4 * h + p))

    def scattered(p, i):
        return remote(moved.at[p, i], moved.at[p, i], sc_s.at[0, 0], sc_r.at[p, i], dev(c_=1 - c))

    def z_moves(*which):
        for up, e in which:
            n = number(up, e)
            p = (l + 8 - e) % 4 if up else (l + e) % 4

            @pl.when(jnp.logical_and(owner, p == y))
            def _():
                z_move(source(e if up else -e, p, side), n, p).start()

            @pl.when(jnp.logical_and(owner, p != y))
            def _():
                scattered(p, rank[up, e]).wait_recv()
                z_move(moved.at[p, rank[up, e]], n, p).start()

    def to_up(n):
        return remote(piece(n, y), piece(n, y), up_y.at[n], nb_r.at[n], dev(y_=y_up))

    def to_dn(n):
        return remote(piece(n, y), piece(n, y), dn_y.at[n], nb_r.at[n], dev(y_=y_dn))

    def from_near(n):
        return piece(n, 2 * c + 1 - side)

    def pass_along(n):
        return remote(from_near(n), from_near(n), rl_s.at[n], rl_r.at[n], dev(y_=y_up if n % 2 else y_dn))

    def passes(n):
        return upward if n % 2 else jnp.logical_not(upward)

    def hand_on(n, j):
        return remote(piece(n, 2 * c + j), piece(n, 2 * c + j), sib_s.at[n, j], sib_r.at[n, j], dev(c_=1 - c))

    def share(*blocks):
        for n in blocks:
            if n in home:
                i = home.index(n)

                @pl.when(jnp.logical_and(owner, y == l))
                def _():
                    stay(i).wait()

                @pl.when(jnp.logical_and(owner, y != l))
                def _():
                    remote(moved.at[0, 0], piece(n, y), sc_s.at[0, 0], sc_r.at[l, i], dev(c_=1 - c)).wait_recv()
            else:
                @pl.when(owner)
                def _():
                    z_move(moved.at[0, 0], n, l).wait_recv()

            @pl.when(owner)
            def _():
                to_up(n).start()
                to_dn(n).start()
                hand_on(n, side).start()

    def relay(*blocks):
        for n in blocks:
            remote(from_near(n), from_near(n), up_y.at[n], nb_r.at[n], dev(c_=1 - c)).wait_recv()

            @pl.when(passes(n))
            def _():
                pass_along(n).start()
            hand_on(n, 1 - side).start()

    def far(*blocks):
        for n in blocks:
            @pl.when(jnp.logical_not(owner))
            def _():
                remote(moved.at[0, 0], piece(n, 2 * c + side), rl_s.at[n], rl_r.at[n], dev(c_=1 - c)).wait_recv()
                hand_on(n, side).start()

    def product(*blocks):
        for n in blocks:
            for j in range(2):
                remote(moved.at[0, 0], piece(n, 2 - 2 * c + j), sib_s.at[n, j], sib_r.at[n, j], dev(c_=1 - c)).wait_recv()

            @pl.loop(0, COLS // TILE)
            def _(j):
                cols = pl.ds(pl.multiple_of(j * TILE, TILE), TILE)
                part[n, :, cols] = jnp.dot(at_all[n], b_all[:, :, cols].reshape(4 * PART, TILE),
                                           preferred_element_type=F32)

    def term(up, f, e):
        return part[number(up, e), :, pl.ds(f * WIDE, WIDE)]

    def hop(up, f, e):
        return remote(send.at[up, f, e - 1], recv.at[up, f, e - 1], rs_s.at[up, f, e - 1], rs_r.at[up, f, e - 1],
                      dev(z_=z_up if up else z_dn))

    def far_side(up, f):
        return up == (1 if f < CHUNKS // 2 else 0)

    def first_hop(up, f, e):
        send[up, f, e - 1] = term(up, f, e).astype(BF)
        hop(up, f, e).start()

    def next_hop(up, f, e):
        mine = term(up, f, e)
        hop(up, f, e + 1).wait_recv()
        send[up, f, e - 1] = (mine + recv[up, f, e].astype(F32)).astype(BF)
        hop(up, f, e).start()

    def hops(e):
        for f in (0, 2, 1, 3):
            for up in ((1, 0) if f < CHUNKS // 2 else (0, 1)):
                if e < REACH - 1 or (e == REACH - 1 and far_side(up, f)):
                    next_hop(up, f, e)
                elif e == REACH - 1 or far_side(up, f):
                    first_hop(up, f, e)

    z_moves((1, 7), (0, 7))
    share(0)
    z_moves((1, 6), (0, 6), (1, 5), (0, 5))
    share(1, 2)
    for up, q in ((1, x_dn), (0, x_up)):
        b_move(q, 1 - up, up, 0).wait_recv()
        b_move(q, 1 - up, up, 2).start()
    relay(0)
    share(3, 4)
    relay(1, 2)
    far(0)
    z_moves((1, 3), (0, 3), (1, 2), (0, 2), (1, 1), (0, 1))
    share(5, 6)
    relay(3, 4)
    far(1, 2)
    share(7, 8)
    relay(5, 6)
    far(3, 4)
    share(9, 10)
    relay(7, 8)
    far(5, 6)

    own_b.wait()
    for up in (1, 0):
        for slot in (1, 2):
            b_move(x, 0, up, slot).wait_recv()

    product(0)
    hops(8)
    share(11, 12)
    relay(9, 10)
    far(7, 8)
    product(1, 2)
    hops(7)
    share(13, 14, 15)
    relay(11, 12)
    far(9, 10)
    product(3, 4)
    hops(6)
    relay(13, 14, 15)
    far(11, 12)
    product(5, 6)
    hops(5)
    far(13, 14, 15)
    product(7, 8)
    hops(4)
    product(9, 10)
    hops(3)
    product(11, 12)
    hops(2)
    product(13, 14)
    hops(1)
    product(15)

    def weights(f, k):
        return wn_ref.at[k, :, pl.ds(f * (WIDE), WIDE)]

    def weights_up(f):
        return remote(weights(f, h), weights(f, h), up_s.at[f], up_r.at[f], dev(z_=z_up4))

    def weights_dn(f):
        return remote(weights(f, h), weights(f, h), dn_s.at[f], dn_r.at[f], dev(z_=z_dn4))

    corr_one = 1.0 - beta_one**adam_step
    corr_two = 1.0 - beta_two**adam_step
    for copy in state:
        copy.wait()
    for f in [0, 2, 1, 3]:
        cols = pl.ds(f * WIDE, WIDE)
        grad = term(1, f, 0)
        for up in (1, 0):
            hop(up, f, 1).wait_recv()
        grad = grad + recv[1, f, 0].astype(F32) + recv[0, f, 0].astype(F32)
        first_next = beta_one * m1_own[:, cols] + (1.0 - beta_one) * grad
        second_next = beta_two * m2_own[:, cols] + (1.0 - beta_two) * grad * grad
        grad_ref[:, cols] = grad
        wide = w_own[:, cols].astype(F32)
        update = (first_next / corr_one / (jnp.sqrt(second_next / corr_two) + epsilon)
                  + decay_rate * wide)
        wn_ref[h, :, cols] = (wide - learn_rate * update).astype(BF)
        (weights_up if f < CHUNKS // 2 else weights_dn)(f).start()
    for f in [0, 2, 1, 3]:
        (weights_dn if f < CHUNKS // 2 else weights_up)(f).start()

    h_dn, h_up, h_far = (h + 3) % 4, (h + 1) % 4, (h + 2) % 4

    def pass_up(f, k):
        return remote(weights(f, k), weights(f, k), fw_s.at[f], fw_r.at[f], dev(z_=z_up4))

    def pass_dn(f, k):
        return remote(weights(f, k), weights(f, k), fw_s.at[f], fw_r.at[f], dev(z_=z_dn4))

    for f in [0, 2, 1, 3]:
        if f < CHUNKS // 2:
            weights_up(f).wait_recv()
            pass_up(f, h_dn).start()
        else:
            weights_dn(f).wait_recv()
            pass_dn(f, h_up).start()
    for f in range(CHUNKS):
        if f < CHUNKS // 2:
            weights_dn(f).wait_recv()
        else:
            weights_up(f).wait_recv()
        pass_up(f, h_far).wait_recv()

    for slot in (0, 1, 2):
        for up in (1, 0):
            b_move(x, 0, up, slot).wait_send()
    for i in range(4):
        for j in range(2):
            @pl.when(2 * c + j != y)
            def _():
                scatter(i, j, False).wait_send()

    @pl.when(owner)
    def _():
        for n in range(RING):
            if n not in home:
                z_move(moved.at[0, 0], n, l).wait_send()
    for n in range(RING):
        @pl.when(owner)
        def _():
            to_up(n).wait_send()
            to_dn(n).wait_send()

        @pl.when(passes(n))
        def _():
            pass_along(n).wait_send()
        for j in range(2):
            hand_on(n, j).wait_send()
    for f in range(CHUNKS):
        weights_up(f).wait_send()
        weights_dn(f).wait_send()
        pass_up(f, 0).wait_send()

    for e in range(1, REACH + 1):
        for f in range(CHUNKS):
            for up in (1, 0):
                if e < REACH or far_side(up, f):
                    hop(up, f, e).wait_send()


def body(inputs, out_grads, weights, first_moment, second_moment):
    vmem = pl.BlockSpec(memory_space=pltpu.VMEM)
    dma = pltpu.SemaphoreType.DMA
    own = first_moment.shape
    grad, weight_next = pl.pallas_call(
        kernel,
        name="adam_grad",
        out_shape=(jax.ShapeDtypeStruct(own, F32),
                   jax.ShapeDtypeStruct((4, ROWS, COLS), BF)),
        in_specs=[pl.BlockSpec(memory_space=pltpu.HBM)] * 5,
        out_specs=(vmem,) * 2,
        scratch_shapes=[
            pltpu.VMEM((4, 4, ROWS, PART), BF),
            pltpu.VMEM((RING, ROWS, 4 * PART), BF),
            pltpu.VMEM((4, PART, COLS), BF),
            pltpu.VMEM((RING, ROWS, COLS), F32),
            pltpu.VMEM((2, CHUNKS, REACH, ROWS, WIDE), BF),
            pltpu.VMEM((2, CHUNKS, REACH, ROWS, WIDE), BF),
            pltpu.VMEM((ROWS, COLS), BF),
            pltpu.VMEM((ROWS, COLS), F32),
            pltpu.VMEM((ROWS, COLS), F32),
            dma((4, 2)), dma((4, 4)), dma((RING,)), dma((RING,)), dma((4,)), dma((4,)),
            dma((RING,)), dma((RING,)), dma((RING,)), dma((RING,)), dma((RING,)),
            dma((RING, 2)), dma((RING, 2)),
            dma((3, 2)), dma((3, 2)),
            dma((2, CHUNKS, REACH)), dma((2, CHUNKS, REACH)),
            dma((CHUNKS,)), dma((CHUNKS,)), dma((CHUNKS,)), dma((CHUNKS,)),
            dma((CHUNKS,)), dma((CHUNKS,)),
        ],
        compiler_params=pltpu.CompilerParams(
            collective_id=0, has_side_effects=True, vmem_limit_bytes=60 * 2**20),
        cost_estimate=pl.CostEstimate(flops=5_700_000_000, bytes_accessed=6_000_000, transcendentals=0),
    )(inputs.T, out_grads, weights, first_moment, second_moment)
    first_next = beta_one * first_moment + (1.0 - beta_one) * grad
    second_next = beta_two * second_moment + (1.0 - beta_two) * grad * grad
    return first_next, second_next, weight_next.reshape(4 * ROWS, COLS)


def solution(mesh):
    in_specs = (
        P(("gy", "gx"), "gz"),
        P(("gy", "gz"), "gx"),
        P(("gz", "gy"), "gx"),
        P(("gz", "gy"), "gx"),
        P(("gz", "gy"), "gx"),
    )
    out_specs = (P(("gz", "gy"), "gx"), P(("gz", "gy"), "gx"), P("gz", "gx"))
    return jax.shard_map(body, mesh=mesh, in_specs=in_specs, out_specs=out_specs, check_vma=False)
```
